32 devices in a mesh: gx: 16 (over z, x, core), gz: 2 (over y).
Axes of the slice: x: 2, y: 2, z: 4, core: 2. Of those that a mesh axis runs over, the one named last changes fastest.
Arguments:
- velocity: float32 [8, 4, 2048, 512], P(None, None, 'gx', 'gz'), may hold values from -130 to 130
- kept: int32 [6], replicated, may hold values from 0 to 7, as said below
- shift: int32 [7], replicated, may hold values from 0 to 64, as said below
Outputs:
- correlation_map: float32 [7, 4, 2048, 512], P(None, None, 'gx', 'gz')
- coefficient: float32 [7, 4], replicated
The draws below stay inside these ranges and needn't reach their ends.
Inputs may be any that keep to these rules, and one draw needn't show every extreme that they name: `kept`: 6 distinct snapshot indices in increasing order. `shift`: not falling with the separation; the shift of the longest separation is 64.
All inputs are finite; a program needn't handle non-finite values.
Results may differ from the reference program's by a relative error of at most 0.0001.
Values sent between devices are 32-bit elements; how exact they have to be, the bound alone decides.
A program may use at most 128 MiB of HBM per device.

```python
import math
import jax
import jax.numpy as jnp
from jax import lax

S = 8
P_SIZE = 4
K = 6
LAGS = 7
SMAX = 64
NX = 2048
NZ = 512


def draw_velocity(key, part):
    key = jax.random.fold_in(key, 11)
    first, second, third = jax.random.split(key, 3)
    ramp = 1.0 + 2.0 * jnp.arange(NX, dtype=jnp.float32) / NX
    row_scale = jnp.exp(jax.random.uniform(second, (S, P_SIZE, NX, 1), jnp.float32, 0.0, math.log(3.2))) * ramp[:, None]
    col_scale = jnp.exp(jax.random.uniform(third, (S, P_SIZE, 1, NZ), jnp.float32, 0.0, math.log(3.2)))
    base = jnp.clip(jax.random.normal(first, (S, P_SIZE, NX, NZ), jnp.float32), -4.0, 4.0)
    return (base * row_scale * col_scale).astype(jnp.float32)


def draw_kept(key, part):
    key = jax.random.fold_in(key, 23)
    order = jax.random.permutation(key, S)[:K]
    return jnp.sort(order).astype(jnp.int32)


def draw_shift(key, part):
    key = jax.random.fold_in(key, 37)
    steps = jnp.arange(LAGS, dtype=jnp.int32)
    reach = max(SMAX // (2 * LAGS), 1)
    jitter = jax.random.randint(key, (LAGS,), 0, reach + 1)
    jitter = jnp.where(steps == LAGS - 1, 0, jitter)
    return ((steps + 1) * SMAX // LAGS - jitter).astype(jnp.int32)


def setup_inputs(seed: int = 0) -> dict:
    seeds = jax.random.split(jax.random.key(seed), 4)
    return {
        "velocity": draw_velocity(jax.random.fold_in(seeds[3], 71), 0),
        "kept": draw_kept(jax.random.fold_in(seeds[3], 71), 0),
        "shift": draw_shift(jax.random.fold_in(seeds[3], 71), 0),
    }


gauss_raw = [math.exp(-k * k / 8.0) for k in range(-4, 5)]
gauss_taps = [v / sum(gauss_raw) for v in gauss_raw]

def smooth(field):
    along_x = jnp.zeros_like(field)
    for index in range(9):
        along_x = along_x + gauss_taps[index] * jnp.roll(field, -(index - 4), axis=2)
    result = jnp.zeros_like(field)
    for index in range(9):
        result = result + gauss_taps[index] * jnp.roll(along_x, -(index - 4), axis=3)
    return result

def reference(velocity, kept, shift):
    filtered = smooth(velocity)
    member = lax.optimization_barrier(jnp.sum((jnp.arange(S)[:, None] == kept[None, :]).astype(jnp.float32), axis=1))
    energy = lax.optimization_barrier(jnp.sum(filtered * filtered, axis=(2, 3))) / (NX * NZ)
    rms = jnp.sqrt(energy + 1e-06)
    scaled = filtered / rms[:, :, None, None]
    maps = []
    for sep in range(1, S):
        weights = member[:S - sep] * member[sep:]
        count = jnp.maximum(jnp.sum(weights), 1.0)
        later = jnp.roll(scaled[sep:], -shift[sep - 1], axis=2)
        total = lax.optimization_barrier(jnp.sum(weights[:, None, None, None] * scaled[:S - sep] * later, axis=0))
        maps.append(total / count)
    correlation_map = jnp.stack(maps, axis=0)
    coefficient = lax.optimization_barrier(jnp.sum(correlation_map, axis=(2, 3))) / (NX * NZ)
    return (correlation_map, coefficient)
```

```python
import functools
import math

import jax
import jax.numpy as jnp
from jax import lax
from jax.experimental import pallas as pl
from jax.experimental.pallas import tpu as pltpu
from jax.sharding import PartitionSpec as P

gauss_raw = [math.exp(-k * k / 8.0) for k in range(-4, 5)]
gauss_taps = [v / sum(gauss_raw) for v in gauss_raw]
MESH = pl.DeviceIdType.MESH
LANES = 128
REACH = 8
f32 = jnp.float32
bf16 = jnp.bfloat16


def tap_of(distance):
    value = jnp.zeros(distance.shape, f32)
    for k in range(5):
        value = jnp.where(distance == k, gauss_taps[4 + k], value)
    return value


def halves(x):
    hi = x.astype(bf16)
    return hi, (x - hi.astype(f32)).astype(bf16)


def remote(src_ref, dst_ref, send, recv, dev):
    return pltpu.make_async_remote_copy(
        src_ref=src_ref, dst_ref=dst_ref, send_sem=send, recv_sem=recv,
        device_id=dev, device_id_type=MESH)


def summed(tile, zbuf, xbuf, rz_send, rz_recv, rx_send, rx_recv):
    gx, gz = lax.axis_index("gx"), lax.axis_index("gz")
    nx, nz = lax.axis_size("gx"), lax.axis_size("gz")
    zbuf[gz] = tile

    def z_copy(k, send):
        k = k if send else nz - k
        who = lax.rem(gz + k, nz)
        at = gz if send else who
        sem = k if send else nz - k
        return remote(zbuf.at[at], zbuf.at[at], rz_send.at[sem], rz_recv.at[sem], (gx, who))

    @pl.loop(1, nz)
    def _(k):
        z_copy(k, True).start()

    @pl.loop(1, nz)
    def _(k):
        z_copy(k, False).wait_recv()

    xbuf[gx] = jnp.sum(zbuf[...], axis=0)

    def x_copy(k, send):
        k = k if send else nx - k
        who = lax.rem(gx + k, nx)
        at = gx if send else who
        sem = k if send else nx - k
        return remote(xbuf.at[at], xbuf.at[at], rx_send.at[sem], rx_recv.at[sem], (who, gz))

    @pl.loop(1, nx)
    def _(k):
        x_copy(k, True).start()

    @pl.loop(1, nx)
    def _(k):
        x_copy(k, False).wait_recv()

    result = jnp.sum(xbuf[...], axis=0)

    @pl.loop(1, nz)
    def _(k):
        z_copy(k, True).wait_send()

    @pl.loop(1, nx)
    def _(k):
        x_copy(k, True).wait_send()

    return result


def taps_x(zb, c, at, size):
    y = gauss_taps[4] * zb[c, at : at + size, :]
    for k in range(1, 5):
        y = y + gauss_taps[4 + k] * (zb[c, at - k : at - k + size, :] + zb[c, at + k : at + k + size, :])
    return y


def exchange(tiles, cells, vel_hbm, kept, shift, fb_hbm, tail_hbm, zx_hbm, inv, vel, fb, tail, zx, hx,
             head_s, head_r, main_s, main_r, up_s, up_r, edge, zh, whi, wlo, zb, eb,
             ez, ex, vel_sem, out_sem, x_send, x_recv, m_send, m_recv, z_send, z_recv,
             rz_send, rz_recv, rx_send, rx_recv):
    snaps, planes, deep, _, cols = vel.shape
    rows = 8 * deep
    nk = kept.shape[0]
    nx, nz = lax.axis_size("gx"), lax.axis_size("gz")
    gx, gz = lax.axis_index("gx"), lax.axis_index("gz")
    xp, xm = lax.rem(gx + 1, nx), lax.rem(gx + nx - 1, nx)
    zp, zm = lax.rem(gz + 1, nz), lax.rem(gz + nz - 1, nz)

    barrier = pltpu.get_barrier_semaphore()

    def greet(dev):
        pl.semaphore_signal(barrier, inc=1, device_id=dev, device_id_type=MESH)

    for dev in ((xm, zm), (xm, zp), (xp, zm), (xp, zp)):
        greet(dev)

    @pl.loop(1, nx)
    def _(k):
        greet((lax.rem(gx + k, nx), gz))

    @pl.loop(1, nz)
    def _(k):
        greet((gx, lax.rem(gz + k, nz)))

    loads = [pltpu.make_async_copy(vel_hbm.at[t], vel.at[t], vel_sem.at[t]) for t in range(snaps)]
    for c in loads:
        c.start()

    src = lax.broadcasted_iota(jnp.int32, (cols + 2 * LANES, cols), 0)
    dst = lax.broadcasted_iota(jnp.int32, (cols + 2 * LANES, cols), 1)
    place = jnp.where(src < cols, src, jnp.where(src < cols + LANES, src % 4 - 4, cols + src % 4))
    weights = tap_of(jnp.abs(place - dst))
    hi, lo = halves(weights)
    whi[...] = hi
    wlo[...] = lo

    reach = []
    start = []
    total = jnp.int32(0)
    for j in range(1, nk):
        s = shift[jnp.clip(kept[j] - kept[0] - 1, 0, snaps - 2)]
        n = (s + 3) // 8
        start.append(total)
        reach.append(n)
        total = total + n

    def source(m):
        j = jnp.int32(1)
        base = start[0]
        for i in range(2, nk):
            later = m >= start[i - 1]
            j = jnp.where(later, i, j)
            base = jnp.where(later, start[i - 1], base)
        return j, jnp.clip(m - base + 1, 1, REACH)

    for c in loads:
        c.wait()

    low = lax.broadcasted_iota(jnp.int32, (8, cols), 0) < 4

    @pl.loop(0, nk)
    def _(j):
        t = kept[j]
        for p in range(planes):
            head_s[j * planes + p] = vel[t, p, 0]
        for p in range(0, planes, 2):
            even = vel[t, p, deep - 1]
            odd = vel[t, p + 1, deep - 1]
            up_s[j * (planes // 2) + p // 2] = jnp.where(low, pltpu.roll(even, 4, 0), odd)

    pl.semaphore_wait(barrier, nx - 1 + nz - 1 + 4)

    head = remote(head_s, head_r, x_send.at[0], x_recv.at[0], (xm, gz))
    head.start()
    upper = remote(up_s, up_r, x_send.at[1], x_recv.at[1], (xp, gz))
    upper.start()

    @pl.loop(0, tiles)
    def _(m):
        j, q = source(m)
        t = kept[j]
        for p in range(planes):
            main_s[p, m] = vel[t, p, q]

    mains = [remote(main_s.at[p], main_r.at[p], m_send.at[p], m_recv.at[p], (xm, gz)) for p in range(planes)]
    mains[0].start()

    lane = lax.broadcasted_iota(jnp.int32, (rows, LANES), 1)
    edge[...] = jnp.zeros(edge.shape, f32)

    @pl.loop(0, nk)
    def _(j):
        t = kept[j]
        left, right = edge[0].reshape(rows, LANES), edge[1].reshape(rows, LANES)
        for p in range(planes):
            m = j * planes + p
            mine = lane // 4 == m
            block = vel[t, p].reshape(rows, cols)
            left = jnp.where(mine, pltpu.roll(block[:, :LANES], 4 * m, 1), left)
            right = jnp.where(mine, pltpu.roll(block[:, cols - LANES :], 4 * m + 4, 1), right)
        edge[0] = left.reshape(deep, 8, LANES)
        edge[1] = right.reshape(deep, 8, LANES)

    zs = []
    for side, (e, dz) in enumerate(((1, zp), (0, zm))):
        for n, (dx, a, size, at) in enumerate(((gx, 0, deep, 1), (xm, 0, REACH + 1, 1 + deep), (xp, deep - 1, 1, 0))):
            zs.append(remote(edge.at[e, pl.ds(a, size)], zh.at[side, pl.ds(at, size)],
                             z_send.at[3 * side + n], z_recv.at[3 * side + n], (dx, dz)))
    for c in zs:
        c.start()
    for c in mains[1:]:
        c.start()

    def along_z(x, sides, mine):
        sides = [jnp.where(mine, side.reshape(x.shape[0], LANES), 0.0) for side in sides]
        a, b = halves(jnp.concatenate([x] + sides, axis=1))
        dot = functools.partial(jnp.dot, preferred_element_type=f32)
        return dot(a, whi[...]) + dot(b, whi[...]) + dot(a, wlo[...])

    def along_x(m, c, first, size):
        y = taps_x(zb, c, first + 8, size)
        fb[m, c, first : first + size, :] = y
        return y

    head.wait_recv()
    upper.wait_recv()
    for c in zs:
        c.wait_recv()

    @pl.loop(0, nk * planes)
    def _(m):
        j, p = m // planes, m % planes
        t = kept[j]
        tile = up_r[m // 2]
        tile = jnp.where(p % 2 == 1, tile, pltpu.roll(tile, 4, 0))
        x = jnp.concatenate([tile, vel[t, p].reshape(rows, cols), head_r[m]], axis=0)
        mine = lax.broadcasted_iota(jnp.int32, (rows + 16, LANES), 1) // 4 == m
        y = along_z(x, [zh[side, : deep + 2] for side in range(2)], mine)
        for c in range(cols // LANES):
            zb[c] = y[:, c * LANES : (c + 1) * LANES]
            tail[m, c] = y[rows:, c * LANES : (c + 1) * LANES]
        energy = jnp.zeros((1, LANES), f32)
        for c in range(cols // LANES):
            for first in range(0, rows, 64):
                y = along_x(m, c, first, 64)
                energy = energy + jnp.sum(y * y, axis=0, keepdims=True)
        eb[pl.ds(m, 1), :] = energy

    lane8 = lax.broadcasted_iota(jnp.int32, (8, LANES), 1)

    tile = jnp.zeros((8, LANES), f32)
    groups = nk * planes // 8
    for g in range(groups):
        part = jnp.sum(eb[8 * g : 8 * g + 8, :], axis=1, keepdims=True)
        tile = jnp.where(lane8 == g, part, tile)
    local = [pltpu.make_async_copy(fb, fb_hbm, out_sem.at[planes]),
             pltpu.make_async_copy(tail, tail_hbm, out_sem.at[planes + 1])]
    for c in local:
        c.start()
    tile = summed(tile, ez, ex, rz_send, rz_recv, rx_send, rx_recv)
    for g in range(groups):
        mean = jnp.sum(jnp.where(lane8 == g, tile, 0.0), axis=1, keepdims=True) / cells
        inv[8 * g : 8 * g + 8, :] = jnp.broadcast_to(1.0 / jnp.sqrt(mean + 1e-06), (8, LANES))

    @pl.loop(0, tiles)
    def _(m):
        j, q = source(m)
        mine = lane8 // (4 * planes) == j
        for side in range(2):
            hx[side, m] = jnp.where(mine, zh[side, deep + 1 + q], 0.0)

    mine = lax.broadcasted_iota(jnp.int32, (8 * tiles, LANES), 1) // 4 % planes
    for p in range(planes):
        mains[p].wait_recv()
        y = along_z(main_r[p].reshape(8 * tiles, cols), [hx[0], hx[1]], mine == p)
        for c in range(cols // LANES):
            zx[p, c] = y[:, c * LANES : (c + 1) * LANES].reshape(tiles, 8, LANES)
        local.append(pltpu.make_async_copy(zx.at[p], zx_hbm.at[p], out_sem.at[p]))
        local[-1].start()

    head.wait_send()
    upper.wait_send()
    for c in zs:
        c.wait_send()
    for c in mains:
        c.wait_send()
    for c in local:
        c.wait()


def correlate(tiles, kept, shift, fb, tail, zx, inv, out, csum, table, pairs, number, zb, gb):
    nk, _, halves_z, rows, _ = fb.shape
    lags = shift.shape[0]
    p = pl.program_id(0)
    planes = pl.num_programs(0)

    @pl.when(p == 0)
    def _():
        for d in range(lags):
            number[d] = 0
        for i in range(nk):
            for j in range(i + 1, nk):
                d = jnp.clip(kept[j] - kept[i] - 1, 0, lags - 1)
                pairs[d, number[d]] = 8 * i + j
                number[d] = number[d] + 1
        total = jnp.int32(0)
        for j in range(1, nk):
            n = (shift[jnp.clip(kept[j] - kept[0] - 1, 0, lags - 1)] + 3) // 8
            table[0, j] = total
            table[1, j] = n
            total = total + n

    for j in range(nk):
        scale = inv[pl.ds(j * planes + p, 1), :]
        for c in range(halves_z):
            gb[j, c, :rows, :] = fb[j, 0, c] * scale

    @pl.loop(1, nk)
    def _(j):
        scale = inv[pl.ds(j * planes + p, 1), :]
        for c in range(halves_z):
            zb[c, 0:16, :] = tail[j, 0, c]
            for q in range(1, REACH + 1):
                at = table[0, j] + jnp.clip(q, 1, jnp.maximum(table[1, j], 1)) - 1
                zb[c, 8 + 8 * q : 16 + 8 * q, :] = zx[0, c, jnp.minimum(at, tiles - 1)]
            gb[j, c, rows:, :] = taps_x(zb, c, 8, 8 * REACH) * scale

    for d in range(lags):
        n = number[d]
        s = shift[d]
        share = 1.0 / jnp.maximum(n, 1).astype(f32)
        part = jnp.zeros((8, LANES), f32)
        for c in range(halves_z):
            for first in range(0, rows, 64):
                def add(i, acc):
                    code = pairs[d, i]
                    a, b = code // 8, code % 8
                    return acc + gb[a, c, first : first + 64, :] * gb[b, c, pl.ds(first + s, 64), :]

                acc = lax.fori_loop(0, n, add, jnp.zeros((64, LANES), f32)) * share
                out[d, 0, first : first + 64, c * LANES : (c + 1) * LANES] = acc
                part = part + jnp.sum(acc.reshape(8, 8, LANES), axis=0)
        csum[0, d] = part
    csum[0, lags] = jnp.zeros((8, LANES), f32)


def means(cells, csum, coef, cz, cx, rz_send, rz_recv, rx_send, rx_recv):
    nx, nz = lax.axis_size("gx"), lax.axis_size("gz")
    gx, gz = lax.axis_index("gx"), lax.axis_index("gz")
    barrier = pltpu.get_barrier_semaphore()

    @pl.loop(1, nx)
    def _(k):
        pl.semaphore_signal(barrier, inc=1, device_id=(lax.rem(gx + k, nx), gz), device_id_type=MESH)

    @pl.loop(1, nz)
    def _(k):
        pl.semaphore_signal(barrier, inc=1, device_id=(gx, lax.rem(gz + k, nz)), device_id_type=MESH)

    lane8 = lax.broadcasted_iota(jnp.int32, (8, LANES), 1)
    tile = jnp.zeros((8, LANES), f32)
    for p in range(csum.shape[0]):
        part = jnp.sum(jnp.sum(csum[p], axis=1), axis=1, keepdims=True)
        tile = jnp.where(lane8 == p, part, tile)
    pl.semaphore_wait(barrier, nx - 1 + nz - 1)
    tile = summed(tile, cz, cx, rz_send, rz_recv, rx_send, rx_recv)
    coef[...] = tile[: coef.shape[0], : coef.shape[1]] / cells


def on_device(velocity, kept, shift):
    snaps, planes, rows, cols = velocity.shape
    nk = kept.shape[0]
    nx, nz = lax.axis_size("gx"), lax.axis_size("gz")
    cells = rows * nx * cols * nz
    tiles = (nk - 1) * REACH
    n = nk * planes
    deep = rows // 8
    wide = cols // LANES
    dma = pltpu.SemaphoreType.DMA
    vmem = pl.BlockSpec(memory_space=pltpu.VMEM)
    smem = pl.BlockSpec(memory_space=pltpu.SMEM)
    anywhere = pl.BlockSpec(memory_space=pl.ANY)
    shape = jax.ShapeDtypeStruct
    sums = [dma((nz,)), dma((nz,)), dma((nx,)), dma((nx,))]
    tiled = velocity.reshape(snaps, planes, deep, 8, cols)
    fb, tail, zx, inv = pl.pallas_call(
        functools.partial(exchange, tiles, cells),
        out_shape=(shape((n, wide, rows, LANES), f32), shape((n, wide, 16, LANES), f32),
                   shape((planes, wide, tiles, 8, LANES), f32), shape((n, LANES), f32)),
        in_specs=[anywhere, smem, smem],
        out_specs=(anywhere, anywhere, anywhere, vmem),
        scratch_shapes=[
            pltpu.VMEM((snaps, planes, deep, 8, cols), f32),
            pltpu.VMEM((n, wide, rows, LANES), f32),
            pltpu.VMEM((n, wide, 16, LANES), f32),
            pltpu.VMEM((planes, wide, tiles, 8, LANES), f32),
            pltpu.VMEM((2, tiles, 8, LANES), f32),
            pltpu.VMEM((n, 8, cols), f32),
            pltpu.VMEM((n, 8, cols), f32),
            pltpu.VMEM((planes, tiles, 8, cols), f32),
            pltpu.VMEM((planes, tiles, 8, cols), f32),
            pltpu.VMEM((n // 2, 8, cols), f32),
            pltpu.VMEM((n // 2, 8, cols), f32),
            pltpu.VMEM((2, deep, 8, LANES), f32),
            pltpu.VMEM((2, deep + REACH + 2, 8, LANES), f32),
            pltpu.VMEM((cols + 2 * LANES, cols), bf16),
            pltpu.VMEM((cols + 2 * LANES, cols), bf16),
            pltpu.VMEM((wide, rows + 16, LANES), f32),
            pltpu.VMEM((n, LANES), f32),
            pltpu.VMEM((nz, 8, LANES), f32),
            pltpu.VMEM((nx, 8, LANES), f32),
            dma((snaps,)), dma((planes + 2,)),
            dma((2,)), dma((2,)), dma((planes,)), dma((planes,)), dma((6,)), dma((6,)),
        ] + sums,
        compiler_params=pltpu.CompilerParams(
            collective_id=0, has_side_effects=True, vmem_limit_bytes=48 * 1024 * 1024),
    )(tiled, kept, shift)
    maps, csum = pl.pallas_call(
        functools.partial(correlate, tiles),
        grid=(planes,),
        out_shape=(shape((snaps - 1, planes, rows, cols), f32), shape((planes, 8, 8, LANES), f32)),
        in_specs=[smem, smem,
                  pl.BlockSpec((nk, 1, wide, rows, LANES), lambda p: (0, p, 0, 0, 0)),
                  pl.BlockSpec((nk, 1, wide, 16, LANES), lambda p: (0, p, 0, 0, 0)),
                  pl.BlockSpec((1, wide, tiles, 8, LANES), lambda p: (p, 0, 0, 0, 0)),
                  pl.BlockSpec((n, LANES), lambda p: (0, 0))],
        out_specs=(pl.BlockSpec((snaps - 1, 1, rows, cols), lambda p: (0, p, 0, 0)),
                   pl.BlockSpec((1, 8, 8, LANES), lambda p: (p, 0, 0, 0))),
        scratch_shapes=[
            pltpu.SMEM((2, 8), jnp.int32),
            pltpu.SMEM((8, 16), jnp.int32),
            pltpu.SMEM((8,), jnp.int32),
            pltpu.VMEM((wide, 16 + 8 * REACH, LANES), f32),
            pltpu.VMEM((nk, wide, rows + 8 * REACH, LANES), f32),
        ],
        compiler_params=pltpu.CompilerParams(vmem_limit_bytes=48 * 1024 * 1024),
    )(kept, shift, fb.reshape(nk, planes, wide, rows, LANES), tail.reshape(nk, planes, wide, 16, LANES), zx, inv)
    coefficient = pl.pallas_call(
        functools.partial(means, cells),
        out_shape=shape((snaps - 1, planes), f32),
        in_specs=[vmem],
        out_specs=vmem,
        scratch_shapes=[pltpu.VMEM((nz, 8, LANES), f32), pltpu.VMEM((nx, 8, LANES), f32)] + sums,
        compiler_params=pltpu.CompilerParams(collective_id=1, has_side_effects=True),
    )(csum)
    return maps, coefficient


def solution(mesh):
    return jax.shard_map(
        on_device,
        mesh=mesh,
        in_specs=(P(None, None, "gx", "gz"), P(), P()),
        out_specs=(P(None, None, "gx", "gz"), P()),
        check_vma=False,
    )
```

```python
import functools
import math

import jax
import jax.numpy as jnp
from jax import lax
from jax.experimental import pallas as pl
from jax.experimental.pallas import tpu as pltpu
from jax.sharding import PartitionSpec as P

gauss_raw = [math.exp(-k * k / 8.0) for k in range(-4, 5)]
gauss_taps = [v / sum(gauss_raw) for v in gauss_raw]
MESH = pl.DeviceIdType.MESH
LANES = 128
REACH = 8
SIZES = [18, 22, 27]
f32 = jnp.float32
bf16 = jnp.bfloat16


def tap_of(distance):
    value = jnp.zeros(distance.shape, f32)
    for k in range(5):
        value = jnp.where(distance == k, gauss_taps[4 + k], value)
    return value


def halves(x):
    hi = x.astype(bf16)
    return hi, (x - hi.astype(f32)).astype(bf16)


def remote(src_ref, dst_ref, send, recv, dev):
    return pltpu.make_async_remote_copy(
        src_ref=src_ref, dst_ref=dst_ref, send_sem=send, recv_sem=recv,
        device_id=dev, device_id_type=MESH)


def summed(tile, zbuf, xbuf, rz_send, rz_recv, rx_send, rx_recv):
    gx, gz = lax.axis_index("gx"), lax.axis_index("gz")
    nx, nz = lax.axis_size("gx"), lax.axis_size("gz")
    zbuf[gz] = tile

    def z_copy(k, send):
        k = k if send else nz - k
        who = lax.rem(gz + k, nz)
        at = gz if send else who
        sem = k if send else nz - k
        return remote(zbuf.at[at], zbuf.at[at], rz_send.at[sem], rz_recv.at[sem], (gx, who))

    @pl.loop(1, nz)
    def _(k):
        z_copy(k, True).start()

    @pl.loop(1, nz)
    def _(k):
        z_copy(k, False).wait_recv()

    xbuf[gx] = jnp.sum(zbuf[...], axis=0)

    def x_copy(k, send):
        k = k if send else nx - k
        who = lax.rem(gx + k, nx)
        at = gx if send else who
        sem = k if send else nx - k
        return remote(xbuf.at[at], xbuf.at[at], rx_send.at[sem], rx_recv.at[sem], (who, gz))

    @pl.loop(1, nx)
    def _(k):
        x_copy(k, True).start()

    @pl.loop(1, nx)
    def _(k):
        x_copy(k, False).wait_recv()

    result = jnp.sum(xbuf[...], axis=0)

    @pl.loop(1, nz)
    def _(k):
        z_copy(k, True).wait_send()

    @pl.loop(1, nx)
    def _(k):
        x_copy(k, True).wait_send()

    return result


def taps_x(zb, c, at, size):
    y = gauss_taps[4] * zb[c, at : at + size, :]
    for k in range(1, 5):
        y = y + gauss_taps[4 + k] * (zb[c, at - k : at - k + size, :] + zb[c, at + k : at + k + size, :])
    return y


def exchange(tiles, cells, vel_hbm, kept, shift, fb_hbm, inv, pair_sum, vel, fb, tail, zx, hx,
             head_s, head_r, main_s, main_r, up_s, up_r, edge, zh, whi, wlo, zb, zc, eb,
             ez, ex, vel_sem, out_sem, x_send, x_recv, m_send, m_recv, z_send, z_recv,
             rz_send, rz_recv, rx_send, rx_recv):
    snaps, planes, deep, _, cols = vel.shape
    rows = 8 * deep
    wide = cols // LANES
    nk = kept.shape[0]
    nx, nz = lax.axis_size("gx"), lax.axis_size("gz")
    gx, gz = lax.axis_index("gx"), lax.axis_index("gz")
    xp, xm = lax.rem(gx + 1, nx), lax.rem(gx + nx - 1, nx)
    zp, zm = lax.rem(gz + 1, nz), lax.rem(gz + nz - 1, nz)

    barrier = pltpu.get_barrier_semaphore()

    def greet(dev):
        pl.semaphore_signal(barrier, inc=1, device_id=dev, device_id_type=MESH)

    for dev in ((xm, zm), (xm, zp), (xp, zm), (xp, zp)):
        greet(dev)

    @pl.loop(1, nx)
    def _(k):
        greet((lax.rem(gx + k, nx), gz))

    @pl.loop(1, nz)
    def _(k):
        greet((gx, lax.rem(gz + k, nz)))

    loads = [pltpu.make_async_copy(vel_hbm.at[t], vel.at[t], vel_sem.at[t]) for t in range(snaps)]
    for c in loads:
        c.start()

    src = lax.broadcasted_iota(jnp.int32, (cols + 2 * LANES, cols), 0)
    dst = lax.broadcasted_iota(jnp.int32, (cols + 2 * LANES, cols), 1)
    place = jnp.where(src < cols, src, jnp.where(src < cols + LANES, src % 4 - 4, cols + src % 4))
    weights = tap_of(jnp.abs(place - dst))
    hi, lo = halves(weights)
    whi[...] = hi
    wlo[...] = lo

    reach = []
    start = []
    total = jnp.int32(0)
    for j in range(1, nk):
        s = shift[jnp.clip(kept[j] - kept[0] - 1, 0, snaps - 2)]
        n = (s + 3) // 8
        start.append(total)
        reach.append(n)
        total = total + n

    def source(m):
        j = jnp.int32(1)
        base = start[0]
        for i in range(2, nk):
            later = m >= start[i - 1]
            j = jnp.where(later, i, j)
            base = jnp.where(later, start[i - 1], base)
        return j, jnp.clip(m - base + 1, 1, REACH)

    for c in loads:
        c.wait()

    low = lax.broadcasted_iota(jnp.int32, (8, cols), 0) < 4

    @pl.loop(0, nk)
    def _(j):
        t = kept[j]
        for p in range(planes):
            head_s[j * planes + p] = vel[t, p, 0]
        for p in range(0, planes, 2):
            even = vel[t, p, deep - 1]
            odd = vel[t, p + 1, deep - 1]
            up_s[j * (planes // 2) + p // 2] = jnp.where(low, pltpu.roll(even, 4, 0), odd)

    pl.semaphore_wait(barrier, nx - 1 + nz - 1 + 4)

    head = remote(head_s, head_r, x_send.at[0], x_recv.at[0], (xm, gz))
    head.start()
    upper = remote(up_s, up_r, x_send.at[1], x_recv.at[1], (xp, gz))
    upper.start()

    @pl.loop(0, tiles)
    def _(m):
        j, q = source(m)
        t = kept[j]
        for p in range(planes):
            main_s[p, m] = vel[t, p, q]

    mains = [remote(main_s.at[p], main_r.at[p], m_send.at[p], m_recv.at[p], (xm, gz)) for p in range(planes)]
    mains[0].start()

    lane = lax.broadcasted_iota(jnp.int32, (rows, LANES), 1)
    edge[...] = jnp.zeros(edge.shape, f32)

    @pl.loop(0, nk)
    def _(j):
        t = kept[j]
        left, right = edge[0].reshape(rows, LANES), edge[1].reshape(rows, LANES)
        for p in range(planes):
            m = j * planes + p
            mine = lane // 4 == m
            block = vel[t, p].reshape(rows, cols)
            left = jnp.where(mine, pltpu.roll(block[:, :LANES], 4 * m, 1), left)
            right = jnp.where(mine, pltpu.roll(block[:, cols - LANES :], 4 * m + 4, 1), right)
        edge[0] = left.reshape(deep, 8, LANES)
        edge[1] = right.reshape(deep, 8, LANES)

    zs = []
    for side, (e, dz) in enumerate(((1, zp), (0, zm))):
        for n, (dx, a, size, at) in enumerate(((gx, 0, deep, 1), (xm, 0, REACH + 1, 1 + deep), (xp, deep - 1, 1, 0))):
            zs.append(remote(edge.at[e, pl.ds(a, size)], zh.at[side, pl.ds(at, size)],
                             z_send.at[3 * side + n], z_recv.at[3 * side + n], (dx, dz)))
    for c in zs:
        c.start()
    for c in mains[1:]:
        c.start()

    def along_z(x, sides, mine):
        sides = [jnp.where(mine, side.reshape(x.shape[0], LANES), 0.0) for side in sides]
        a, b = halves(jnp.concatenate([x] + sides, axis=1))
        dot = functools.partial(jnp.dot, preferred_element_type=f32)
        return dot(a, whi[...]) + dot(b, whi[...]) + dot(a, wlo[...])

    head.wait_recv()
    upper.wait_recv()
    for c in zs:
        c.wait_recv()

    @pl.loop(0, nk)
    def _(j):
        t = kept[j]
        for p in range(planes):
            m = j * planes + p
            tile = up_r[j * (planes // 2) + p // 2]
            tile = tile if p % 2 == 1 else pltpu.roll(tile, 4, 0)
            x = jnp.concatenate([tile, vel[t, p].reshape(rows, cols), head_r[m]], axis=0)
            mine = lax.broadcasted_iota(jnp.int32, (rows + 16, LANES), 1) // 4 == m
            y = along_z(x, [zh[side, : deep + 2] for side in range(2)], mine)
            for c in range(wide):
                zb[p, c] = y[:, c * LANES : (c + 1) * LANES]
                tail[m, c] = y[rows:, c * LANES : (c + 1) * LANES]
        for p in range(planes):
            m = j * planes + p
            energy = jnp.zeros((1, LANES), f32)
            for c in range(wide):
                y = taps_x(zb.at[p], c, 8, rows)
                fb[m, c, :deep] = y.reshape(deep, 8, LANES)
                energy = energy + jnp.sum(y * y, axis=0, keepdims=True)
            eb[pl.ds(m, 1), :] = energy

    lane8 = lax.broadcasted_iota(jnp.int32, (8, LANES), 1)

    @pl.loop(0, tiles)
    def _(m):
        j, q = source(m)
        mine = lane8 // (4 * planes) == j
        for side in range(2):
            hx[side, m] = jnp.where(mine, zh[side, deep + 1 + q], 0.0)

    owner = lax.broadcasted_iota(jnp.int32, (8 * tiles, LANES), 1) // 4 % planes
    sub = lax.broadcasted_iota(jnp.int32, (deep, 8, LANES), 1)
    pairs = [(a, b) for a in range(nk) for b in range(a + 1, nk)]
    eb[pl.ds(nk * planes + len(pairs) * planes, 4), :] = jnp.zeros((4, LANES), f32)

    @pl.loop(0, planes)
    def _(p):
        remote(main_s.at[p], main_r.at[p], m_send.at[p], m_recv.at[p], (xm, gz)).wait_recv()
        y = along_z(main_r[p].reshape(8 * tiles, cols), [hx[0], hx[1]], owner == p)
        for c in range(wide):
            zx[c] = y[:, c * LANES : (c + 1) * LANES].reshape(tiles, 8, LANES)
        for j in range(1, nk):
            m = j * planes + p
            for c in range(wide):
                zc[j - 1, c, 0:16, :] = tail[m, c]
                for q in range(1, REACH + 1):
                    at = start[j - 1] + jnp.clip(q, 1, jnp.maximum(reach[j - 1], 1)) - 1
                    zc[j - 1, c, 8 + 8 * q : 16 + 8 * q, :] = zx[c, jnp.clip(at, 0, tiles - 1)]
            for c in range(wide):
                fb[m, c, deep:] = taps_x(zc.at[j - 1], c, 8, 8 * REACH).reshape(REACH, 8, LANES)
        for n, (a, b) in enumerate(pairs):
            s = shift[jnp.clip(kept[b] - kept[a] - 1, 0, snaps - 2)]
            whole, rest = s // 8, s % 8
            total = jnp.zeros((8, LANES), f32)
            for c in range(wide):
                later = jnp.stack([fb[b * planes + p, c, jnp.clip(q + whole, 0, deep + REACH - 1)]
                                   for q in range(deep + 1)])
                later = pltpu.roll(later, (8 - rest) % 8, 1)
                later = jnp.where(sub < 8 - rest, later[:deep], later[1:])
                total = total + jnp.sum(fb[a * planes + p, c, :deep] * later, axis=0)
            eb[pl.ds(planes * (nk + n) + p, 1), :] = jnp.sum(total, axis=0, keepdims=True)

    local = pltpu.make_async_copy(fb, fb_hbm, out_sem.at[0])
    local.start()
    tile = jnp.zeros((8, LANES), f32)
    groups = eb.shape[0] // 8
    for g in range(groups):
        part = jnp.sum(eb[8 * g : 8 * g + 8, :], axis=1, keepdims=True)
        tile = jnp.where(lane8 == g, part, tile)
    tile = summed(tile, ez, ex, rz_send, rz_recv, rx_send, rx_recv)
    for g in range(groups):
        mean = jnp.sum(jnp.where(lane8 == g, tile, 0.0), axis=1, keepdims=True) / cells
        mean = jnp.broadcast_to(mean, (8, LANES))
        if 8 * g < nk * planes:
            inv[8 * g : 8 * g + 8, :] = 1.0 / jnp.sqrt(mean + 1e-06)
        else:
            at = 8 * g - nk * planes
            pair_sum[at : at + 8, :] = mean

    head.wait_send()
    upper.wait_send()
    for c in zs:
        c.wait_send()
    for c in mains:
        c.wait_send()
    local.wait()


def correlate(kept, shift, fb, inv, pair_sum, out, coef, pairs, number):
    nk, _, wide, _, _ = fb.shape
    rows = out.shape[2]
    lags = shift.shape[0]
    p = pl.program_id(0)
    planes = pl.num_programs(0)

    @pl.when(p == 0)
    def _():
        for d in range(lags):
            number[d] = 0
        n = 0
        for i in range(nk):
            for j in range(i + 1, nk):
                d = jnp.clip(kept[j] - kept[i] - 1, 0, lags - 1)
                pairs[d, number[d]] = 64 * n + 8 * i + j
                number[d] = number[d] + 1
                n += 1

    lane = lax.broadcasted_iota(jnp.int32, (1, LANES), 1)
    means = jnp.zeros((1, LANES), f32)
    for d in range(lags):
        n = number[d]
        s = shift[d]
        share = 1.0 / jnp.maximum(n, 1).astype(f32)

        def add(i, carry):
            code = pairs[d, i]
            a, b = code // 8 % 8, code % 8
            scale = inv[pl.ds(a * planes + p, 1), :] * inv[pl.ds(b * planes + p, 1), :] * share
            mean = carry[0] + pair_sum[pl.ds(code // 64 * planes + p, 1), :] * scale
            return (mean,) + tuple(
                carry[1 + c] + (fb[a, 0, c, :rows, :] * scale) * fb[b, 0, c, pl.ds(s, rows), :] for c in range(wide))

        zero = jnp.zeros((rows, LANES), f32)
        mean, *maps = lax.fori_loop(0, n, add, (jnp.zeros((1, LANES), f32),) + (zero,) * wide)
        for c in range(wide):
            out[d, 0, :, c * LANES : (c + 1) * LANES] = maps[c]
        means = jnp.where(lane == d, mean, means)
    coef[pl.ds(p, 1), :] = means[:, :lags]


def on_device(velocity, kept, shift):
    snaps, planes, rows, cols = velocity.shape
    nk = kept.shape[0]
    nx, nz = lax.axis_size("gx"), lax.axis_size("gz")
    cells = rows * nx * cols * nz
    n = nk * planes
    deep = rows // 8
    wide = cols // LANES
    dma = pltpu.SemaphoreType.DMA
    vmem = pl.BlockSpec(memory_space=pltpu.VMEM)
    smem = pl.BlockSpec(memory_space=pltpu.SMEM)
    anywhere = pl.BlockSpec(memory_space=pl.ANY)
    shape = jax.ShapeDtypeStruct
    tiled = velocity.reshape(snaps, planes, deep, 8, cols)
    count = planes * nk * (nk - 1) // 2
    sums = -(-(n + count) // 8) * 8

    def exchanged(tiles, number):
        return pl.pallas_call(
            functools.partial(exchange, tiles, cells),
            out_shape=(shape((n, wide, deep + REACH, 8, LANES), f32), shape((n, LANES), f32),
                       shape((sums - n, LANES), f32)),
            in_specs=[anywhere, smem, smem],
            out_specs=(anywhere, vmem, vmem),
            scratch_shapes=[
                pltpu.VMEM((snaps, planes, deep, 8, cols), f32),
                pltpu.VMEM((n, wide, deep + REACH, 8, LANES), f32),
                pltpu.VMEM((n, wide, 16, LANES), f32),
                pltpu.VMEM((wide, tiles, 8, LANES), f32),
                pltpu.VMEM((2, tiles, 8, LANES), f32),
                pltpu.VMEM((n, 8, cols), f32),
                pltpu.VMEM((n, 8, cols), f32),
                pltpu.VMEM((planes, tiles, 8, cols), f32),
                pltpu.VMEM((planes, tiles, 8, cols), f32),
                pltpu.VMEM((n // 2, 8, cols), f32),
                pltpu.VMEM((n // 2, 8, cols), f32),
                pltpu.VMEM((2, deep, 8, LANES), f32),
                pltpu.VMEM((2, deep + REACH + 2, 8, LANES), f32),
                pltpu.VMEM((cols + 2 * LANES, cols), bf16),
                pltpu.VMEM((cols + 2 * LANES, cols), bf16),
                pltpu.VMEM((planes, wide, rows + 16, LANES), f32),
                pltpu.VMEM((nk - 1, wide, 16 + 8 * REACH, LANES), f32),
                pltpu.VMEM((sums, LANES), f32),
                pltpu.VMEM((nz, 8, LANES), f32),
                pltpu.VMEM((nx, 8, LANES), f32),
                dma((snaps,)), dma((1,)),
                dma((2,)), dma((2,)), dma((planes,)), dma((planes,)), dma((6,)), dma((6,)),
                dma((nz,)), dma((nz,)), dma((nx,)), dma((nx,)),
            ],
            compiler_params=pltpu.CompilerParams(
                collective_id=number, has_side_effects=True, vmem_limit_bytes=48 * 1024 * 1024),
        )

    sizes = SIZES + [(nk - 1) * REACH]
    needed = jnp.int32(0)
    for d in range(1, snaps):
        inside = jnp.any(kept - kept[0] == d)
        needed = needed + jnp.where(inside, (shift[d - 1] + 3) >> 3, 0)
    branch = sum((needed > size).astype(jnp.int32) for size in sizes[:-1])
    if len(sizes) == 1:
        fb, inv, pair_sum = exchanged(sizes[0], 0)(tiled, kept, shift)
    else:
        fb, inv, pair_sum = lax.switch(
            branch, [exchanged(size, number) for number, size in enumerate(sizes)], tiled, kept, shift)
    maps, coefficient = pl.pallas_call(
        correlate,
        grid=(planes,),
        out_shape=(shape((snaps - 1, planes, rows, cols), f32), shape((planes, snaps - 1), f32)),
        in_specs=[smem, smem,
                  pl.BlockSpec((nk, 1, wide, rows + 8 * REACH, LANES), lambda p: (0, p, 0, 0, 0)),
                  pl.BlockSpec((n, LANES), lambda p: (0, 0)),
                  pl.BlockSpec((sums - n, LANES), lambda p: (0, 0))],
        out_specs=(pl.BlockSpec((snaps - 1, 1, rows, cols), lambda p: (0, p, 0, 0)),
                   pl.BlockSpec((planes, snaps - 1), lambda p: (0, 0))),
        scratch_shapes=[pltpu.SMEM((8, 16), jnp.int32), pltpu.SMEM((8,), jnp.int32)],
        compiler_params=pltpu.CompilerParams(vmem_limit_bytes=48 * 1024 * 1024),
    )(kept, shift, fb.reshape(nk, planes, wide, rows + 8 * REACH, LANES), inv, pair_sum)
    return maps, coefficient.T


def solution(mesh):
    return jax.shard_map(
        on_device,
        mesh=mesh,
        in_specs=(P(None, None, "gx", "gz"), P(), P()),
        out_specs=(P(None, None, "gx", "gz"), P()),
        check_vma=False,
    )
```

```python
import functools
import math

import jax
import jax.numpy as jnp
from jax import lax
from jax.experimental import pallas as pl
from jax.experimental.pallas import tpu as pltpu
from jax.sharding import PartitionSpec as P

gauss_raw = [math.exp(-k * k / 8.0) for k in range(-4, 5)]
gauss_taps = [v / sum(gauss_raw) for v in gauss_raw]
MESH = pl.DeviceIdType.MESH
LANES = 128
REACH = 8
SIZES = []
f32 = jnp.float32
bf16 = jnp.bfloat16


def tap_of(distance):
    value = jnp.zeros(distance.shape, f32)
    for k in range(5):
        value = jnp.where(distance == k, gauss_taps[4 + k], value)
    return value


def halves(x):
    hi = x.astype(bf16)
    return hi, (x - hi.astype(f32)).astype(bf16)


def remote(src_ref, dst_ref, send, recv, dev):
    return pltpu.make_async_remote_copy(
        src_ref=src_ref, dst_ref=dst_ref, send_sem=send, recv_sem=recv,
        device_id=dev, device_id_type=MESH)


def summed(tile, zbuf, xbuf, rz_send, rz_recv, rx_send, rx_recv):
    gx, gz = lax.axis_index("gx"), lax.axis_index("gz")
    nx, nz = lax.axis_size("gx"), lax.axis_size("gz")
    zbuf[gz] = tile

    def z_copy(k, send):
        k = k if send else nz - k
        who = lax.rem(gz + k, nz)
        at = gz if send else who
        sem = k if send else nz - k
        return remote(zbuf.at[at], zbuf.at[at], rz_send.at[sem], rz_recv.at[sem], (gx, who))

    @pl.loop(1, nz)
    def _(k):
        z_copy(k, True).start()

    @pl.loop(1, nz)
    def _(k):
        z_copy(k, False).wait_recv()

    xbuf[gx] = jnp.sum(zbuf[...], axis=0)

    def x_copy(k, send):
        k = k if send else nx - k
        who = lax.rem(gx + k, nx)
        at = gx if send else who
        sem = k if send else nx - k
        return remote(xbuf.at[at], xbuf.at[at], rx_send.at[sem], rx_recv.at[sem], (who, gz))

    @pl.loop(1, nx)
    def _(k):
        x_copy(k, True).start()

    @pl.loop(1, nx)
    def _(k):
        x_copy(k, False).wait_recv()

    result = jnp.sum(xbuf[...], axis=0)

    @pl.loop(1, nz)
    def _(k):
        z_copy(k, True).wait_send()

    @pl.loop(1, nx)
    def _(k):
        x_copy(k, True).wait_send()

    return result


def taps_x(zb, c, at, size):
    y = gauss_taps[4] * zb[c, at : at + size, :]
    for k in range(1, 5):
        y = y + gauss_taps[4 + k] * (zb[c, at - k : at - k + size, :] + zb[c, at + k : at + k + size, :])
    return y


def exchange(tiles, cells, vel_hbm, kept, shift, fb_hbm, inv, pair_sum, vel, fb, tail, zx, hx,
             head_s, head_r, main_s, main_r, up_s, up_r, edge, zh, whi, wlo, zb, zc, eb,
             ez, ex, vel_sem, out_sem, x_send, x_recv, m_send, m_recv, z_send, z_recv,
             rz_send, rz_recv, rx_send, rx_recv):
    snaps, planes, deep, _, cols = vel.shape
    rows = 8 * deep
    wide = cols // LANES
    nk = kept.shape[0]
    nx, nz = lax.axis_size("gx"), lax.axis_size("gz")
    gx, gz = lax.axis_index("gx"), lax.axis_index("gz")
    xp, xm = lax.rem(gx + 1, nx), lax.rem(gx + nx - 1, nx)
    zp, zm = lax.rem(gz + 1, nz), lax.rem(gz + nz - 1, nz)

    barrier = pltpu.get_barrier_semaphore()

    def greet(dev):
        pl.semaphore_signal(barrier, inc=1, device_id=dev, device_id_type=MESH)

    for dev in ((xm, zm), (xm, zp), (xp, zm), (xp, zp)):
        greet(dev)

    @pl.loop(1, nx)
    def _(k):
        greet((lax.rem(gx + k, nx), gz))

    @pl.loop(1, nz)
    def _(k):
        greet((gx, lax.rem(gz + k, nz)))

    loads = [pltpu.make_async_copy(vel_hbm.at[t], vel.at[t], vel_sem.at[t]) for t in range(snaps)]
    for c in loads:
        c.start()

    src = lax.broadcasted_iota(jnp.int32, (cols + 2 * LANES, cols), 0)
    dst = lax.broadcasted_iota(jnp.int32, (cols + 2 * LANES, cols), 1)
    place = jnp.where(src < cols, src, jnp.where(src < cols + LANES, src % 4 - 4, cols + src % 4))
    weights = tap_of(jnp.abs(place - dst))
    hi, lo = halves(weights)
    whi[...] = hi
    wlo[...] = lo

    reach = []
    start = []
    total = jnp.int32(0)
    for j in range(1, nk):
        s = shift[jnp.clip(kept[j] - kept[0] - 1, 0, snaps - 2)]
        n = (s + 3) // 8
        start.append(total)
        reach.append(n)
        total = total + n

    def source(m):
        j = jnp.int32(1)
        base = start[0]
        for i in range(2, nk):
            later = m >= start[i - 1]
            j = jnp.where(later, i, j)
            base = jnp.where(later, start[i - 1], base)
        return j, jnp.clip(m - base + 1, 1, REACH)

    for c in loads:
        c.wait()

    low = lax.broadcasted_iota(jnp.int32, (8, cols), 0) < 4

    @pl.loop(0, nk)
    def _(j):
        t = kept[j]
        for p in range(planes):
            head_s[j * planes + p] = vel[t, p, 0]
        for p in range(0, planes, 2):
            even = vel[t, p, deep - 1]
            odd = vel[t, p + 1, deep - 1]
            up_s[j * (planes // 2) + p // 2] = jnp.where(low, pltpu.roll(even, 4, 0), odd)

    pl.semaphore_wait(barrier, nx - 1 + nz - 1 + 4)

    head = remote(head_s, head_r, x_send.at[0], x_recv.at[0], (xm, gz))
    head.start()
    upper = remote(up_s, up_r, x_send.at[1], x_recv.at[1], (xp, gz))
    upper.start()

    @pl.loop(0, tiles)
    def _(m):
        j, q = source(m)
        t = kept[j]
        for p in range(planes):
            main_s[p, m] = vel[t, p, q]

    mains = [remote(main_s.at[p], main_r.at[p], m_send.at[p], m_recv.at[p], (xm, gz)) for p in range(planes)]
    mains[0].start()

    lane = lax.broadcasted_iota(jnp.int32, (rows, LANES), 1)
    edge[...] = jnp.zeros(edge.shape, f32)

    @pl.loop(0, nk)
    def _(j):
        t = kept[j]
        left, right = edge[0].reshape(rows, LANES), edge[1].reshape(rows, LANES)
        for p in range(planes):
            m = j * planes + p
            mine = lane // 4 == m
            block = vel[t, p].reshape(rows, cols)
            left = jnp.where(mine, pltpu.roll(block[:, :LANES], 4 * m, 1), left)
            right = jnp.where(mine, pltpu.roll(block[:, cols - LANES :], 4 * m + 4, 1), right)
        edge[0] = left.reshape(deep, 8, LANES)
        edge[1] = right.reshape(deep, 8, LANES)

    zs = []
    for side, (e, dz) in enumerate(((1, zp), (0, zm))):
        for n, (dx, a, size, at) in enumerate(((gx, 0, deep, 1), (xm, 0, REACH + 1, 1 + deep), (xp, deep - 1, 1, 0))):
            zs.append(remote(edge.at[e, pl.ds(a, size)], zh.at[side, pl.ds(at, size)],
                             z_send.at[3 * side + n], z_recv.at[3 * side + n], (dx, dz)))
    for c in zs:
        c.start()
    for c in mains[1:]:
        c.start()

    def along_z(x, sides, mine):
        sides = [jnp.where(mine, side.reshape(x.shape[0], LANES), 0.0) for side in sides]
        a, b = halves(jnp.concatenate([x] + sides, axis=1))
        dot = functools.partial(jnp.dot, preferred_element_type=f32)
        return dot(a, whi[...]) + dot(b, whi[...]) + dot(a, wlo[...])

    head.wait_recv()
    upper.wait_recv()
    for c in zs:
        c.wait_recv()

    @pl.loop(0, nk)
    def _(j):
        t = kept[j]
        for p in range(planes):
            m = j * planes + p
            tile = up_r[j * (planes // 2) + p // 2]
            tile = tile if p % 2 == 1 else pltpu.roll(tile, 4, 0)
            x = jnp.concatenate([tile, vel[t, p].reshape(rows, cols), head_r[m]], axis=0)
            mine = lax.broadcasted_iota(jnp.int32, (rows + 16, LANES), 1) // 4 == m
            y = along_z(x, [zh[side, : deep + 2] for side in range(2)], mine)
            for c in range(wide):
                zb[p, c] = y[:, c * LANES : (c + 1) * LANES]
                tail[m, c] = y[rows:, c * LANES : (c + 1) * LANES]
        for p in range(planes):
            m = j * planes + p
            energy = jnp.zeros((1, LANES), f32)
            for c in range(wide):
                y = taps_x(zb.at[p], c, 8, rows)
                fb[m, c, :deep] = y.reshape(deep, 8, LANES)
                energy = energy + jnp.sum(y * y, axis=0, keepdims=True)
            eb[pl.ds(m, 1), :] = energy

    lane8 = lax.broadcasted_iota(jnp.int32, (8, LANES), 1)

    @pl.loop(0, tiles)
    def _(m):
        j, q = source(m)
        mine = lane8 // (4 * planes) == j
        for side in range(2):
            hx[side, m] = jnp.where(mine, zh[side, deep + 1 + q], 0.0)

    owner = lax.broadcasted_iota(jnp.int32, (8 * tiles, LANES), 1) // 4 % planes
    sub = lax.broadcasted_iota(jnp.int32, (deep, 8, LANES), 1)
    pairs = [(a, b) for a in range(nk) for b in range(a + 1, nk)]
    eb[pl.ds(nk * planes + len(pairs) * planes, 4), :] = jnp.zeros((4, LANES), f32)

    @pl.loop(0, planes)
    def _(p):
        remote(main_s.at[p], main_r.at[p], m_send.at[p], m_recv.at[p], (xm, gz)).wait_recv()
        y = along_z(main_r[p].reshape(8 * tiles, cols), [hx[0], hx[1]], owner == p)
        for c in range(wide):
            zx[c] = y[:, c * LANES : (c + 1) * LANES].reshape(tiles, 8, LANES)
        for j in range(1, nk):
            m = j * planes + p
            for c in range(wide):
                zc[j - 1, c, 0:16, :] = tail[m, c]
                for q in range(1, REACH + 1):
                    at = start[j - 1] + jnp.clip(q, 1, jnp.maximum(reach[j - 1], 1)) - 1
                    zc[j - 1, c, 8 + 8 * q : 16 + 8 * q, :] = zx[c, jnp.clip(at, 0, tiles - 1)]
            for c in range(wide):
                fb[m, c, deep:] = taps_x(zc.at[j - 1], c, 8, 8 * REACH).reshape(REACH, 8, LANES)
        for n, (a, b) in enumerate(pairs):
            s = shift[jnp.clip(kept[b] - kept[a] - 1, 0, snaps - 2)]
            whole, rest = s // 8, s % 8
            total = jnp.zeros((8, LANES), f32)
            for c in range(wide):
                later = jnp.stack([fb[b * planes + p, c, jnp.clip(q + whole, 0, deep + REACH - 1)]
                                   for q in range(deep + 1)])
                later = pltpu.roll(later, (8 - rest) % 8, 1)
                later = jnp.where(sub < 8 - rest, later[:deep], later[1:])
                total = total + jnp.sum(fb[a * planes + p, c, :deep] * later, axis=0)
            eb[pl.ds(planes * (nk + n) + p, 1), :] = jnp.sum(total, axis=0, keepdims=True)

    local = pltpu.make_async_copy(fb, fb_hbm, out_sem.at[0])
    local.start()
    tile = jnp.zeros((8, LANES), f32)
    groups = eb.shape[0] // 8
    for g in range(groups):
        part = jnp.sum(eb[8 * g : 8 * g + 8, :], axis=1, keepdims=True)
        tile = jnp.where(lane8 == g, part, tile)
    tile = summed(tile, ez, ex, rz_send, rz_recv, rx_send, rx_recv)
    for g in range(groups):
        mean = jnp.sum(jnp.where(lane8 == g, tile, 0.0), axis=1, keepdims=True) / cells
        mean = jnp.broadcast_to(mean, (8, LANES))
        if 8 * g < nk * planes:
            inv[8 * g : 8 * g + 8, :] = 1.0 / jnp.sqrt(mean + 1e-06)
        else:
            at = 8 * g - nk * planes
            pair_sum[at : at + 8, :] = mean

    head.wait_send()
    upper.wait_send()
    for c in zs:
        c.wait_send()
    for c in mains:
        c.wait_send()
    local.wait()


def correlate(kept, shift, fb, inv, pair_sum, out, coef, pairs, number):
    nk, _, wide, _, _ = fb.shape
    rows = out.shape[2]
    lags = shift.shape[0]
    p = pl.program_id(0)
    planes = pl.num_programs(0)

    @pl.when(p == 0)
    def _():
        for d in range(lags):
            number[d] = 0
        n = 0
        for i in range(nk):
            for j in range(i + 1, nk):
                d = jnp.clip(kept[j] - kept[i] - 1, 0, lags - 1)
                pairs[d, number[d]] = 64 * n + 8 * i + j
                number[d] = number[d] + 1
                n += 1

    lane = lax.broadcasted_iota(jnp.int32, (1, LANES), 1)
    means = jnp.zeros((1, LANES), f32)
    for d in range(lags):
        n = number[d]
        s = shift[d]
        share = 1.0 / jnp.maximum(n, 1).astype(f32)

        def add(i, carry):
            code = pairs[d, i]
            a, b = code // 8 % 8, code % 8
            scale = inv[pl.ds(a * planes + p, 1), :] * inv[pl.ds(b * planes + p, 1), :] * share
            mean = carry[0] + pair_sum[pl.ds(code // 64 * planes + p, 1), :] * scale
            return (mean,) + tuple(
                carry[1 + c] + (fb[a, 0, c, :rows, :] * scale) * fb[b, 0, c, pl.ds(s, rows), :] for c in range(wide))

        zero = jnp.zeros((rows, LANES), f32)
        mean, *maps = lax.fori_loop(0, n, add, (jnp.zeros((1, LANES), f32),) + (zero,) * wide)
        for c in range(wide):
            out[d, 0, :, c * LANES : (c + 1) * LANES] = maps[c]
        means = jnp.where(lane == d, mean, means)
    coef[pl.ds(p, 1), :] = means[:, :lags]


def on_device(velocity, kept, shift):
    snaps, planes, rows, cols = velocity.shape
    nk = kept.shape[0]
    nx, nz = lax.axis_size("gx"), lax.axis_size("gz")
    cells = rows * nx * cols * nz
    n = nk * planes
    deep = rows // 8
    wide = cols // LANES
    dma = pltpu.SemaphoreType.DMA
    vmem = pl.BlockSpec(memory_space=pltpu.VMEM)
    smem = pl.BlockSpec(memory_space=pltpu.SMEM)
    anywhere = pl.BlockSpec(memory_space=pl.ANY)
    shape = jax.ShapeDtypeStruct
    tiled = velocity.reshape(snaps, planes, deep, 8, cols)
    count = planes * nk * (nk - 1) // 2
    sums = -(-(n + count) // 8) * 8

    def exchanged(tiles, number):
        return pl.pallas_call(
            functools.partial(exchange, tiles, cells),
            out_shape=(shape((n, wide, deep + REACH, 8, LANES), f32), shape((n, LANES), f32),
                       shape((sums - n, LANES), f32)),
            in_specs=[anywhere, smem, smem],
            out_specs=(anywhere, vmem, vmem),
            scratch_shapes=[
                pltpu.VMEM((snaps, planes, deep, 8, cols), f32),
                pltpu.VMEM((n, wide, deep + REACH, 8, LANES), f32),
                pltpu.VMEM((n, wide, 16, LANES), f32),
                pltpu.VMEM((wide, tiles, 8, LANES), f32),
                pltpu.VMEM((2, tiles, 8, LANES), f32),
                pltpu.VMEM((n, 8, cols), f32),
                pltpu.VMEM((n, 8, cols), f32),
                pltpu.VMEM((planes, tiles, 8, cols), f32),
                pltpu.VMEM((planes, tiles, 8, cols), f32),
                pltpu.VMEM((n // 2, 8, cols), f32),
                pltpu.VMEM((n // 2, 8, cols), f32),
                pltpu.VMEM((2, deep, 8, LANES), f32),
                pltpu.VMEM((2, deep + REACH + 2, 8, LANES), f32),
                pltpu.VMEM((cols + 2 * LANES, cols), bf16),
                pltpu.VMEM((cols + 2 * LANES, cols), bf16),
                pltpu.VMEM((planes, wide, rows + 16, LANES), f32),
                pltpu.VMEM((nk - 1, wide, 16 + 8 * REACH, LANES), f32),
                pltpu.VMEM((sums, LANES), f32),
                pltpu.VMEM((nz, 8, LANES), f32),
                pltpu.VMEM((nx, 8, LANES), f32),
                dma((snaps,)), dma((1,)),
                dma((2,)), dma((2,)), dma((planes,)), dma((planes,)), dma((6,)), dma((6,)),
                dma((nz,)), dma((nz,)), dma((nx,)), dma((nx,)),
            ],
            compiler_params=pltpu.CompilerParams(
                collective_id=number, has_side_effects=True, vmem_limit_bytes=48 * 1024 * 1024),
        )

    sizes = SIZES + [(nk - 1) * REACH]
    needed = jnp.int32(0)
    for d in range(1, snaps):
        inside = jnp.any(kept - kept[0] == d)
        needed = needed + jnp.where(inside, (shift[d - 1] + 3) >> 3, 0)
    branch = sum((needed > size).astype(jnp.int32) for size in sizes[:-1])
    if len(sizes) == 1:
        fb, inv, pair_sum = exchanged(sizes[0], 0)(tiled, kept, shift)
    else:
        fb, inv, pair_sum = lax.switch(
            branch, [exchanged(size, number) for number, size in enumerate(sizes)], tiled, kept, shift)
    maps, coefficient = pl.pallas_call(
        correlate,
        grid=(planes,),
        out_shape=(shape((snaps - 1, planes, rows, cols), f32), shape((planes, snaps - 1), f32)),
        in_specs=[smem, smem,
                  pl.BlockSpec((nk, 1, wide, rows + 8 * REACH, LANES), lambda p: (0, p, 0, 0, 0)),
                  pl.BlockSpec((n, LANES), lambda p: (0, 0)),
                  pl.BlockSpec((sums - n, LANES), lambda p: (0, 0))],
        out_specs=(pl.BlockSpec((snaps - 1, 1, rows, cols), lambda p: (0, p, 0, 0)),
                   pl.BlockSpec((planes, snaps - 1), lambda p: (0, 0))),
        scratch_shapes=[pltpu.SMEM((8, 16), jnp.int32), pltpu.SMEM((8,), jnp.int32)],
        compiler_params=pltpu.CompilerParams(vmem_limit_bytes=48 * 1024 * 1024),
    )(kept, shift, fb.reshape(nk, planes, wide, rows + 8 * REACH, LANES), inv, pair_sum)
    return maps, coefficient.T


def solution(mesh):
    return jax.shard_map(
        on_device,
        mesh=mesh,
        in_specs=(P(None, None, "gx", "gz"), P(), P()),
        out_specs=(P(None, None, "gx", "gz"), P()),
        check_vma=False,
    )
```

```python
import functools
import math

import jax
import jax.numpy as jnp
from jax import lax
from jax.experimental import pallas as pl
from jax.experimental.pallas import tpu as pltpu
from jax.sharding import PartitionSpec as P

gauss_raw = [math.exp(-k * k / 8.0) for k in range(-4, 5)]
gauss_taps = [v / sum(gauss_raw) for v in gauss_raw]
MESH = pl.DeviceIdType.MESH
LANES = 128
REACH = 8
SIZES = []
f32 = jnp.float32
bf16 = jnp.bfloat16


def tap_of(distance):
    value = jnp.zeros(distance.shape, f32)
    for k in range(5):
        value = jnp.where(distance == k, gauss_taps[4 + k], value)
    return value


def halves(x):
    hi = x.astype(bf16)
    return hi, (x - hi.astype(f32)).astype(bf16)


def remote(src_ref, dst_ref, send, recv, dev):
    return pltpu.make_async_remote_copy(
        src_ref=src_ref, dst_ref=dst_ref, send_sem=send, recv_sem=recv,
        device_id=dev, device_id_type=MESH)


def summed(tile, zbuf, xbuf, rz_send, rz_recv, rx_send, rx_recv):
    gx, gz = lax.axis_index("gx"), lax.axis_index("gz")
    nx, nz = lax.axis_size("gx"), lax.axis_size("gz")
    zbuf[gz] = tile

    def z_copy(k, send):
        k = k if send else nz - k
        who = lax.rem(gz + k, nz)
        at = gz if send else who
        sem = k if send else nz - k
        return remote(zbuf.at[at], zbuf.at[at], rz_send.at[sem], rz_recv.at[sem], (gx, who))

    @pl.loop(1, nz)
    def _(k):
        z_copy(k, True).start()

    @pl.loop(1, nz)
    def _(k):
        z_copy(k, False).wait_recv()

    xbuf[gx] = jnp.sum(zbuf[...], axis=0)

    def x_copy(k, send):
        k = k if send else nx - k
        who = lax.rem(gx + k, nx)
        at = gx if send else who
        sem = k if send else nx - k
        return remote(xbuf.at[at], xbuf.at[at], rx_send.at[sem], rx_recv.at[sem], (who, gz))

    @pl.loop(1, nx)
    def _(k):
        x_copy(k, True).start()

    @pl.loop(1, nx)
    def _(k):
        x_copy(k, False).wait_recv()

    result = jnp.sum(xbuf[...], axis=0)

    @pl.loop(1, nz)
    def _(k):
        z_copy(k, True).wait_send()

    @pl.loop(1, nx)
    def _(k):
        x_copy(k, True).wait_send()

    return result


def taps_x(zb, c, at, size):
    y = gauss_taps[4] * zb[c, at : at + size, :]
    for k in range(1, 5):
        y = y + gauss_taps[4 + k] * (zb[c, at - k : at - k + size, :] + zb[c, at + k : at + k + size, :])
    return y


def exchange(tiles, cells, vel_hbm, kept, shift, fb_hbm, inv, pair_sum, vel, fb, tail, zx, hx,
             head_s, head_r, main_s, main_r, up_s, up_r, edge, zh, whi, wlo, zb, zc, eb,
             ez, ex, vel_sem, out_sem, x_send, x_recv, m_send, m_recv, z_send, z_recv,
             rz_send, rz_recv, rx_send, rx_recv):
    snaps, planes, deep, _, cols = vel.shape
    rows = 8 * deep
    wide = cols // LANES
    nk = kept.shape[0]
    nx, nz = lax.axis_size("gx"), lax.axis_size("gz")
    gx, gz = lax.axis_index("gx"), lax.axis_index("gz")
    xp, xm = lax.rem(gx + 1, nx), lax.rem(gx + nx - 1, nx)
    zp, zm = lax.rem(gz + 1, nz), lax.rem(gz + nz - 1, nz)

    barrier = pltpu.get_barrier_semaphore()

    def greet(dev):
        pl.semaphore_signal(barrier, inc=1, device_id=dev, device_id_type=MESH)

    for dev in ((xm, zm), (xm, zp), (xp, zm), (xp, zp)):
        greet(dev)

    @pl.loop(1, nx)
    def _(k):
        greet((lax.rem(gx + k, nx), gz))

    @pl.loop(1, nz)
    def _(k):
        greet((gx, lax.rem(gz + k, nz)))

    loads = [pltpu.make_async_copy(vel_hbm.at[t], vel.at[t], vel_sem.at[t]) for t in range(snaps)]
    for c in loads:
        c.start()

    src = lax.broadcasted_iota(jnp.int32, (cols + 2 * LANES, cols), 0)
    dst = lax.broadcasted_iota(jnp.int32, (cols + 2 * LANES, cols), 1)
    place = jnp.where(src < cols, src, jnp.where(src < cols + LANES, src % 4 - 4, cols + src % 4))
    weights = tap_of(jnp.abs(place - dst))
    hi, lo = halves(weights)
    whi[...] = hi
    wlo[...] = lo

    reach = []
    start = []
    total = jnp.int32(0)
    for j in range(1, nk):
        s = shift[jnp.clip(kept[j] - kept[0] - 1, 0, snaps - 2)]
        n = (s + 3) // 8
        start.append(total)
        reach.append(n)
        total = total + n

    def source(m):
        j = jnp.int32(1)
        base = start[0]
        for i in range(2, nk):
            later = m >= start[i - 1]
            j = jnp.where(later, i, j)
            base = jnp.where(later, start[i - 1], base)
        return j, jnp.clip(m - base + 1, 1, REACH)

    for c in loads:
        c.wait()

    low = lax.broadcasted_iota(jnp.int32, (8, cols), 0) < 4

    @pl.loop(0, nk)
    def _(j):
        t = kept[j]
        for p in range(planes):
            head_s[j * planes + p] = vel[t, p, 0]
        for p in range(0, planes, 2):
            even = vel[t, p, deep - 1]
            odd = vel[t, p + 1, deep - 1]
            up_s[j * (planes // 2) + p // 2] = jnp.where(low, pltpu.roll(even, 4, 0), odd)

    pl.semaphore_wait(barrier, nx - 1 + nz - 1 + 4)

    head = remote(head_s, head_r, x_send.at[0], x_recv.at[0], (xm, gz))
    head.start()
    upper = remote(up_s, up_r, x_send.at[1], x_recv.at[1], (xp, gz))
    upper.start()

    @pl.loop(0, tiles)
    def _(m):
        j, q = source(m)
        t = kept[j]
        for p in range(planes):
            main_s[p, m] = vel[t, p, q]

    mains = [remote(main_s.at[p], main_r.at[p], m_send.at[p], m_recv.at[p], (xm, gz)) for p in range(planes)]
    mains[0].start()

    lane = lax.broadcasted_iota(jnp.int32, (rows, LANES), 1)
    edge[...] = jnp.zeros(edge.shape, f32)

    @pl.loop(0, nk)
    def _(j):
        t = kept[j]
        left, right = edge[0].reshape(rows, LANES), edge[1].reshape(rows, LANES)
        for p in range(planes):
            m = j * planes + p
            mine = lane // 4 == m
            block = vel[t, p].reshape(rows, cols)
            left = jnp.where(mine, pltpu.roll(block[:, :LANES], 4 * m, 1), left)
            right = jnp.where(mine, pltpu.roll(block[:, cols - LANES :], 4 * m + 4, 1), right)
        edge[0] = left.reshape(deep, 8, LANES)
        edge[1] = right.reshape(deep, 8, LANES)

    zs = []
    for side, (e, dz) in enumerate(((1, zp), (0, zm))):
        for n, (dx, a, size, at) in enumerate(((gx, 0, deep, 1), (xm, 0, REACH + 1, 1 + deep), (xp, deep - 1, 1, 0))):
            zs.append(remote(edge.at[e, pl.ds(a, size)], zh.at[side, pl.ds(at, size)],
                             z_send.at[3 * side + n], z_recv.at[3 * side + n], (dx, dz)))
    for c in zs:
        c.start()
    for c in mains[1:]:
        c.start()

    def along_z(x, sides, mine):
        sides = [jnp.where(mine, side.reshape(x.shape[0], LANES), 0.0) for side in sides]
        a, b = halves(jnp.concatenate([x] + sides, axis=1))
        dot = functools.partial(jnp.dot, preferred_element_type=f32)
        return dot(a, whi[...]) + dot(b, whi[...]) + dot(a, wlo[...])

    head.wait_recv()
    upper.wait_recv()
    for c in zs:
        c.wait_recv()

    @pl.loop(0, nk)
    def _(j):
        t = kept[j]
        for p in range(planes):
            m = j * planes + p
            tile = up_r[j * (planes // 2) + p // 2]
            tile = tile if p % 2 == 1 else pltpu.roll(tile, 4, 0)
            x = jnp.concatenate([tile, vel[t, p].reshape(rows, cols), head_r[m]], axis=0)
            mine = lax.broadcasted_iota(jnp.int32, (rows + 16, LANES), 1) // 4 == m
            y = along_z(x, [zh[side, : deep + 2] for side in range(2)], mine)
            for c in range(wide):
                zb[p, c] = y[:, c * LANES : (c + 1) * LANES]
                tail[m, c] = y[rows:, c * LANES : (c + 1) * LANES]
        for p in range(planes):
            m = j * planes + p
            energy = jnp.zeros((1, LANES), f32)
            for c in range(wide):
                y = taps_x(zb.at[p], c, 8, rows)
                fb[m, c, :deep] = y.reshape(deep, 8, LANES)
                energy = energy + jnp.sum(y * y, axis=0, keepdims=True)
            eb[pl.ds(m, 1), :] = energy

    lane8 = lax.broadcasted_iota(jnp.int32, (8, LANES), 1)

    @pl.loop(0, tiles)
    def _(m):
        j, q = source(m)
        mine = lane8 // (4 * planes) == j
        for side in range(2):
            hx[side, m] = jnp.where(mine, zh[side, deep + 1 + q], 0.0)

    owner = lax.broadcasted_iota(jnp.int32, (8 * tiles, LANES), 1) // 4 % planes
    sub = lax.broadcasted_iota(jnp.int32, (deep, 8, LANES), 1)
    pairs = [(a, b) for a in range(nk) for b in range(a + 1, nk)]
    eb[pl.ds(nk * planes + len(pairs) * planes, 4), :] = jnp.zeros((4, LANES), f32)

    @pl.loop(0, planes)
    def _(p):
        remote(main_s.at[p], main_r.at[p], m_send.at[p], m_recv.at[p], (xm, gz)).wait_recv()
        y = along_z(main_r[p].reshape(8 * tiles, cols), [hx[0], hx[1]], owner == p)
        for c in range(wide):
            zx[c] = y[:, c * LANES : (c + 1) * LANES].reshape(tiles, 8, LANES)
        for j in range(1, nk):
            m = j * planes + p
            for c in range(wide):
                zc[j - 1, c, 0:16, :] = tail[m, c]
                for q in range(1, REACH + 1):
                    at = start[j - 1] + jnp.clip(q, 1, jnp.maximum(reach[j - 1], 1)) - 1
                    zc[j - 1, c, 8 + 8 * q : 16 + 8 * q, :] = zx[c, jnp.clip(at, 0, tiles - 1)]
            for c in range(wide):
                fb[m, c, deep:] = taps_x(zc.at[j - 1], c, 8, 8 * REACH).reshape(REACH, 8, LANES)
        for n, (a, b) in enumerate(pairs):
            s = shift[jnp.clip(kept[b] - kept[a] - 1, 0, snaps - 2)]
            whole, rest = s // 8, s % 8
            total = jnp.zeros((8, LANES), f32)
            for c in range(wide):
                later = jnp.stack([fb[b * planes + p, c, jnp.clip(q + whole, 0, deep + REACH - 1)]
                                   for q in range(deep + 1)])
                later = pltpu.roll(later, (8 - rest) % 8, 1)
                later = jnp.where(sub < 8 - rest, later[:deep], later[1:])
                total = total + jnp.sum(fb[a * planes + p, c, :deep] * later, axis=0)
            eb[pl.ds(planes * (nk + n) + p, 1), :] = jnp.sum(total, axis=0, keepdims=True)

    local = pltpu.make_async_copy(fb, fb_hbm, out_sem.at[0])
    local.start()
    tile = jnp.zeros((8, LANES), f32)
    groups = eb.shape[0] // 8
    for g in range(groups):
        part = jnp.sum(eb[8 * g : 8 * g + 8, :], axis=1, keepdims=True)
        tile = jnp.where(lane8 == g, part, tile)
    tile = summed(tile, ez, ex, rz_send, rz_recv, rx_send, rx_recv)
    for g in range(groups):
        mean = jnp.sum(jnp.where(lane8 == g, tile, 0.0), axis=1, keepdims=True) / cells
        mean = jnp.broadcast_to(mean, (8, LANES))
        if 8 * g < nk * planes:
            inv[8 * g : 8 * g + 8, :] = 1.0 / jnp.sqrt(mean + 1e-06)
        else:
            at = 8 * g - nk * planes
            pair_sum[at : at + 8, :] = mean

    head.wait_send()
    upper.wait_send()
    for c in zs:
        c.wait_send()
    for c in mains:
        c.wait_send()
    local.wait()


def correlate(kept, shift, fb, inv, pair_sum, out, coef, pairs, number):
    nk, _, wide, _, _ = fb.shape
    rows = out.shape[2]
    lags = shift.shape[0]
    p = pl.program_id(0)
    planes = pl.num_programs(0)

    @pl.when(p == 0)
    def _():
        for d in range(lags):
            number[d] = 0
        n = 0
        for i in range(nk):
            for j in range(i + 1, nk):
                d = jnp.clip(kept[j] - kept[i] - 1, 0, lags - 1)
                pairs[d, number[d]] = 64 * n + 8 * i + j
                number[d] = number[d] + 1
                n += 1

    lane = lax.broadcasted_iota(jnp.int32, (1, LANES), 1)
    means = jnp.zeros((1, LANES), f32)
    for d in range(lags):
        n = number[d]
        s = shift[d]
        share = 1.0 / jnp.maximum(n, 1).astype(f32)

        def add(i, carry):
            code = pairs[d, i]
            a, b = code // 8 % 8, code % 8
            scale = inv[pl.ds(a * planes + p, 1), :] * inv[pl.ds(b * planes + p, 1), :] * share
            mean = carry[0] + pair_sum[pl.ds(code // 64 * planes + p, 1), :] * scale
            return (mean,) + tuple(
                carry[1 + c] + (fb[a, 0, c, :rows, :] * scale) * fb[b, 0, c, pl.ds(s, rows), :] for c in range(wide))

        zero = jnp.zeros((rows, LANES), f32)
        mean, *maps = lax.fori_loop(0, n, add, (jnp.zeros((1, LANES), f32),) + (zero,) * wide)
        for c in range(wide):
            out[d, 0, :, c * LANES : (c + 1) * LANES] = maps[c]
        means = jnp.where(lane == d, mean, means)
    coef[pl.ds(p, 1), :] = means[:, :lags]


def on_device(velocity, kept, shift):
    snaps, planes, rows, cols = velocity.shape
    nk = kept.shape[0]
    nx, nz = lax.axis_size("gx"), lax.axis_size("gz")
    cells = rows * nx * cols * nz
    n = nk * planes
    deep = rows // 8
    wide = cols // LANES
    dma = pltpu.SemaphoreType.DMA
    vmem = pl.BlockSpec(memory_space=pltpu.VMEM)
    smem = pl.BlockSpec(memory_space=pltpu.SMEM)
    anywhere = pl.BlockSpec(memory_space=pl.ANY)
    shape = jax.ShapeDtypeStruct
    tiled = velocity.reshape(snaps, planes, deep, 8, cols)
    count = planes * nk * (nk - 1) // 2
    sums = -(-(n + count) // 8) * 8

    def exchanged(tiles, number):
        return pl.pallas_call(
            functools.partial(exchange, tiles, cells),
            out_shape=(shape((n, wide, deep + REACH, 8, LANES), f32), shape((n, LANES), f32),
                       shape((sums - n, LANES), f32)),
            in_specs=[anywhere, smem, smem],
            out_specs=(anywhere, vmem, vmem),
            scratch_shapes=[
                pltpu.VMEM((snaps, planes, deep, 8, cols), f32),
                pltpu.VMEM((n, wide, deep + REACH, 8, LANES), f32),
                pltpu.VMEM((n, wide, 16, LANES), f32),
                pltpu.VMEM((wide, tiles, 8, LANES), f32),
                pltpu.VMEM((2, tiles, 8, LANES), f32),
                pltpu.VMEM((n, 8, cols), f32),
                pltpu.VMEM((n, 8, cols), f32),
                pltpu.VMEM((planes, tiles, 8, cols), f32),
                pltpu.VMEM((planes, tiles, 8, cols), f32),
                pltpu.VMEM((n // 2, 8, cols), f32),
                pltpu.VMEM((n // 2, 8, cols), f32),
                pltpu.VMEM((2, deep, 8, LANES), f32),
                pltpu.VMEM((2, deep + REACH + 2, 8, LANES), f32),
                pltpu.VMEM((cols + 2 * LANES, cols), bf16),
                pltpu.VMEM((cols + 2 * LANES, cols), bf16),
                pltpu.VMEM((planes, wide, rows + 16, LANES), f32),
                pltpu.VMEM((nk - 1, wide, 16 + 8 * REACH, LANES), f32),
                pltpu.VMEM((sums, LANES), f32),
                pltpu.VMEM((nz, 8, LANES), f32),
                pltpu.VMEM((nx, 8, LANES), f32),
                dma((snaps,)), dma((1,)),
                dma((2,)), dma((2,)), dma((planes,)), dma((planes,)), dma((6,)), dma((6,)),
                dma((nz,)), dma((nz,)), dma((nx,)), dma((nx,)),
            ],
            compiler_params=pltpu.CompilerParams(
                collective_id=number, has_side_effects=True, vmem_limit_bytes=60 * 1024 * 1024),
        )

    sizes = SIZES + [(nk - 1) * REACH]
    needed = jnp.int32(0)
    for d in range(1, snaps):
        inside = jnp.any(kept - kept[0] == d)
        needed = needed + jnp.where(inside, (shift[d - 1] + 3) >> 3, 0)
    branch = sum((needed > size).astype(jnp.int32) for size in sizes[:-1])
    if len(sizes) == 1:
        fb, inv, pair_sum = exchanged(sizes[0], 0)(tiled, kept, shift)
    else:
        fb, inv, pair_sum = lax.switch(
            branch, [exchanged(size, number) for number, size in enumerate(sizes)], tiled, kept, shift)
    maps, coefficient = pl.pallas_call(
        correlate,
        grid=(planes,),
        out_shape=(shape((snaps - 1, planes, rows, cols), f32), shape((planes, snaps - 1), f32)),
        in_specs=[smem, smem,
                  pl.BlockSpec((nk, 1, wide, rows + 8 * REACH, LANES), lambda p: (0, p, 0, 0, 0)),
                  pl.BlockSpec((n, LANES), lambda p: (0, 0)),
                  pl.BlockSpec((sums - n, LANES), lambda p: (0, 0))],
        out_specs=(pl.BlockSpec((snaps - 1, 1, rows, cols), lambda p: (0, p, 0, 0)),
                   pl.BlockSpec((planes, snaps - 1), lambda p: (0, 0))),
        scratch_shapes=[pltpu.SMEM((8, 16), jnp.int32), pltpu.SMEM((8,), jnp.int32)],
        compiler_params=pltpu.CompilerParams(vmem_limit_bytes=60 * 1024 * 1024),
    )(kept, shift, fb.reshape(nk, planes, wide, rows + 8 * REACH, LANES), inv, pair_sum)
    return maps, coefficient.T


def solution(mesh):
    return jax.shard_map(
        on_device,
        mesh=mesh,
        in_specs=(P(None, None, "gx", "gz"), P(), P()),
        out_specs=(P(None, None, "gx", "gz"), P()),
        check_vma=False,
    )
```
